32 devices in a mesh: ctx: 8 (over z, y), tp: 4 (over x, core).
Axes of the slice: x: 2, y: 2, z: 4, core: 2. Of those that a mesh axis runs over, the one named last changes fastest.
Arguments:
- query: bfloat16 [2048, 4096], P('ctx', 'tp'), may hold values from -96 to 96
- key: bfloat16 [2048, 4096], P('ctx', 'tp'), may hold values from -4 to 4
- value: bfloat16 [2048, 4096], P('ctx', 'tp'), may hold values from -6 to 6
- xin: bfloat16 [2048, 4096], P('ctx', 'tp'), may hold values from -1 to 8
- gate_z: bfloat16 [2048, 4096], P('ctx', 'tp'), may hold values from -6 to 6
- w_bc: bfloat16 [4096, 32], P('tp'), may hold values from -1 to 1
- dt_low: bfloat16 [2048, 256], P('ctx'), may hold values from -4 to 9
- dt_proj: bfloat16 [256, 4096], P(None, 'tp'), may hold values from -3 to 3
- dt_bias: float32 [4096], P('tp'), may hold values from -20 to 0
- a_rate: float32 [16, 4096], P(None, 'tp'), may hold values from 1 to 16
- skip: float32 [4096], P('tp'), may hold values from 0.2 to 2
Outputs:
- attended: bfloat16 [2048, 4096], P('ctx', 'tp')
- mixed: bfloat16 [2048, 4096], P('ctx', 'tp')
The draws below stay inside these ranges and needn't reach their ends.
All inputs are finite; a program needn't handle non-finite values.
Results may differ from the reference program's by a relative error of at most 0.0085.
Values may be sent and summed in bfloat16 or wider, within the bound.
A program may use at most 128 MiB of HBM per device.

```python
import math
import jax
import jax.numpy as jnp
from jax import lax

HEADS = 32
HD = 128
WINDOW = 2048
CH = 4096
NS = 16
DT_RANK = 256
TOK_DEV = 256
STRING_LENGTH = 2048


def drawn_rows(key):
    key_rows = jnp.clip(jax.random.normal(jax.random.fold_in(key, 101), (STRING_LENGTH, HEADS * HD), jnp.float32), -4.0, 4.0)
    return key_rows


def draw_key(key, part):
    key_rows = drawn_rows(key)
    return key_rows.astype(jnp.bfloat16)


def draw_query(key, part):
    queries = 2.5 * jnp.clip(jax.random.normal(jax.random.fold_in(key, 103), (STRING_LENGTH, HEADS * HD), jnp.float32), -6.0, 6.0)
    return queries.astype(jnp.bfloat16)


def draw_xin(key, part):
    raw_vals = 2.0 * jnp.clip(jax.random.normal(jax.random.fold_in(key, 201), (STRING_LENGTH, CH), jnp.float32), -4.0, 4.0)
    return jax.nn.silu(raw_vals).astype(jnp.bfloat16)


def draw_w_bc(key, part):
    base_vals = jnp.clip(jax.random.normal(jax.random.fold_in(key, 301), (CH, 2 * NS), jnp.float32), -6.0, 6.0) / math.sqrt(CH)
    signs = jnp.where(jax.random.bernoulli(jax.random.fold_in(key, 302), 0.5, (NS,)), 1.0, -1.0)
    magnitude = jax.random.uniform(jax.random.fold_in(key, 303), (NS,), jnp.float32, 0.5, 1.5)
    offsets = jnp.concatenate([signs * magnitude * 2.0 / CH, jnp.zeros((NS,), jnp.float32)])
    return (base_vals + offsets[None, :]).astype(jnp.bfloat16)


def draw_dt_low(key, part):
    entry_indices = jnp.arange(STRING_LENGTH)
    packet_bundles = jax.random.randint(jax.random.fold_in(key, 401), (8,), 0, STRING_LENGTH)
    packet_slot = jnp.where(jnp.any(entry_indices[:, None] == packet_bundles[None, :], axis=1), 9.0, 0.0)
    block_vals = jax.random.uniform(jax.random.fold_in(key, 402), (STRING_LENGTH // TOK_DEV,), jnp.float32, -1.0, 1.0)
    worker_slot = block_vals[entry_indices // TOK_DEV]
    leftover_entries = jnp.clip(jax.random.normal(jax.random.fold_in(key, 403), (STRING_LENGTH, DT_RANK - 2), jnp.float32), -4.0, 4.0)
    merged_result = jnp.concatenate([packet_slot[:, None], worker_slot[:, None], leftover_entries], axis=1)
    return merged_result.astype(jnp.bfloat16)


def draw_dt_proj(key, part):
    first_row = jax.random.uniform(jax.random.fold_in(key, 501), (1, CH), jnp.float32, 0.95, 1.05)
    second_row = jax.random.uniform(jax.random.fold_in(key, 502), (1, CH), jnp.float32, -0.8, 0.8)
    leftover_entries = jnp.clip(jax.random.normal(jax.random.fold_in(key, 503), (DT_RANK - 2, CH), jnp.float32), -4.0, 4.0) * (0.6 / math.sqrt(DT_RANK - 2))
    return jnp.concatenate([first_row, second_row, leftover_entries], axis=0).astype(jnp.bfloat16)


def draw_dt_bias(key, part):
    slow_share = 0.5
    chooser = jax.random.uniform(jax.random.fold_in(key, 601), (CH,), jnp.float32)
    slow_vals = -jnp.log(jax.random.uniform(jax.random.fold_in(key, 602), (CH,), jnp.float32, 2.0, 6.0) * STRING_LENGTH)
    fast_vals = -jax.random.uniform(jax.random.fold_in(key, 603), (CH,), jnp.float32, math.log(24.0), math.log(max(48.0, 2.0 * TOK_DEV)))
    return jnp.where(chooser < slow_share, slow_vals, fast_vals).astype(jnp.float32)


def level_of(stream_key, extent, shards, least, largest):
    factor_of = 1.0
    for axis_at, shards_of in shards:
        steps = jax.random.uniform(jax.random.fold_in(jax.random.fold_in(stream_key, 6), axis_at), (shards_of,), jnp.float32, least / len(shards), largest / len(shards))
        factor_of = factor_of * jnp.repeat(jnp.exp(steps), extent[axis_at] // shards_of).reshape((-1,) + (1,) * (len(extent) - 1 - axis_at))
    return factor_of


def noise(own_key, dims, scale, most, pieces=(), kind=jnp.bfloat16):
    array = jax.random.normal(own_key, dims, jnp.float32) * scale
    if len(pieces) > 0:
        array = level_of(own_key, dims, pieces, -0.22, 0.18) * array
    return jnp.clip(array, min=-most, max=most).astype(kind)


def setup_inputs(seed: int = 0) -> dict:
    keys = jax.random.split(jax.random.key(seed), 12)
    return {
        "query": draw_query(jax.random.fold_in(keys[11], 71), 0),
        "key": draw_key(jax.random.fold_in(keys[11], 71), 0),
        "value": noise(keys[2], (STRING_LENGTH, HEADS * HD), 1.0, 6.0, ((0, 8), (1, 4))),
        "xin": draw_xin(jax.random.fold_in(keys[11], 71), 0),
        "gate_z": noise(keys[4], (STRING_LENGTH, CH), 1.0, 6.0, ((0, 8), (1, 4))),
        "w_bc": draw_w_bc(jax.random.fold_in(keys[11], 71), 0),
        "dt_low": draw_dt_low(jax.random.fold_in(keys[11], 71), 0),
        "dt_proj": draw_dt_proj(jax.random.fold_in(keys[11], 71), 0),
        "dt_bias": draw_dt_bias(jax.random.fold_in(keys[11], 71), 0),
        "a_rate": jnp.clip(jnp.exp(math.log(16.0) - 2.7725887 * jax.random.uniform(keys[9], (NS, CH), jnp.float32) ** level_of(keys[9], (NS, CH), ((1, 4),), -0.2, 0.2)), 1.0, 16.0),
        "skip": jnp.clip(jnp.exp(math.log(2.0) - 2.3025851 * jax.random.uniform(keys[10], (CH,), jnp.float32) ** level_of(keys[10], (CH,), ((0, 4),), -0.2, 0.2)), 0.2, 2.0),
    }


def attention_part(query, key, value):
    block_len = TOK_DEV
    padding = jnp.zeros((WINDOW, HEADS * HD), jnp.bfloat16)
    key_padded = jnp.concatenate([padding, key], axis=0)
    value_padded = jnp.concatenate([padding, value], axis=0)
    scale = HD ** -0.5

    def one_block(block_id):
        start = (block_id * block_len).astype(jnp.int32)
        q_rows = lax.dynamic_slice_in_dim(query, start, block_len, 0).reshape(block_len, HEADS, HD).astype(jnp.float32)
        k_rows = lax.dynamic_slice_in_dim(key_padded, start, WINDOW + block_len, 0).reshape(WINDOW + block_len, HEADS, HD).astype(jnp.float32)
        v_rows = lax.dynamic_slice_in_dim(value_padded, start, WINDOW + block_len, 0).reshape(WINDOW + block_len, HEADS, HD).astype(jnp.float32)
        scores = jnp.einsum("qhd,khd->hqk", q_rows, k_rows) * scale
        query_pos = start + jnp.arange(block_len, dtype=jnp.int32)
        key_pos = start - WINDOW + jnp.arange(WINDOW + block_len, dtype=jnp.int32)
        allowed = (key_pos[None, :] <= query_pos[:, None]) & (key_pos[None, :] > query_pos[:, None] - WINDOW) & (key_pos[None, :] >= 0)
        masked = jnp.where(allowed[None], scores, -jnp.inf)
        row_max = jnp.max(masked, axis=2, keepdims=True)
        unscaled = jnp.where(allowed[None], jnp.exp(scores - row_max), 0.0)
        row_sum = jnp.sum(unscaled, axis=2, keepdims=True)
        probs = (unscaled / row_sum).astype(jnp.bfloat16)
        output = jnp.einsum("hqk,khd->qhd", probs.astype(jnp.float32), v_rows)
        return output.reshape(block_len, HEADS * HD).astype(jnp.bfloat16)

    blocks = lax.map(one_block, jnp.arange(STRING_LENGTH // block_len, dtype=jnp.int32))
    return blocks.reshape(STRING_LENGTH, HEADS * HD)


def reference(query, key, value, xin, gate_z, w_bc, dt_low, dt_proj, dt_bias, a_rate, skip):
    attended = attention_part(query, key, value)
    summed_bc = jnp.dot(xin, w_bc, preferred_element_type=jnp.float32)
    b_rows = summed_bc[:, :NS]
    c_rows = summed_bc[:, NS:]
    step_sizes = jax.nn.softplus(jnp.dot(dt_low, dt_proj, preferred_element_type=jnp.float32) + dt_bias[None, :])

    def advance(carried, inputs):
        step_row, input_row, b_vec, c_vec, gate_row = inputs
        input_f = input_row.astype(jnp.float32)
        driven = step_row * input_f
        carried = jnp.exp(-step_row[None, :] * a_rate) * carried + driven[None, :] * b_vec[:, None]
        output = jnp.sum(c_vec[:, None] * carried, axis=0) + skip * input_f
        gated = output * jax.nn.silu(gate_row.astype(jnp.float32))
        return carried, gated.astype(jnp.bfloat16)

    start_state = jnp.zeros((NS, CH), jnp.float32)
    last_state, mixed = lax.scan(advance, start_state, (step_sizes, xin, b_rows, c_rows, gate_z))
    return attended, mixed
```

```python
import functools
import math

import jax
import jax.numpy as jnp
from jax import lax
from jax.experimental import pallas as pl
from jax.experimental.pallas import tpu as pltpu
from jax.sharding import PartitionSpec as P

HD = 128
WINDOW = 2048
NS = 16
LANES = 128
SUB = 8
LOG2E = math.log2(math.e)
RADIX = 8
VMEM = pl.BlockSpec(memory_space=pltpu.VMEM)
SMEM = pl.BlockSpec(memory_space=pltpu.SMEM)
PARAMS = pltpu.CompilerParams(vmem_limit_bytes=40 * 1024 * 1024)


def shifted(block, axis, distance):
    peers = lax.axis_size(axis)
    return lax.ppermute(block, axis, [(i, i + distance) for i in range(peers - distance)])


def rotated(block, axis, group, distance):
    peers = lax.axis_size(axis)
    route = [(i, i // group * group + (i % group + distance) % group) for i in range(peers)]
    return lax.ppermute(block, axis, route)


def head_at(group, distance):
    slot = lax.rem(lax.axis_index("ctx"), group)
    return lax.rem(slot + distance + group, group)


def pack_kernel(group, q_ref, k_ref, v_ref, *outs):
    for d in range(group):
        col = pl.ds(pl.multiple_of(head_at(group, d) * HD, HD), HD)
        for part, ref in enumerate((q_ref, k_ref, v_ref)):
            outs[d][part] = ref[:, col]


def pack(query, key, value, group):
    rows = query.shape[0]
    return pl.pallas_call(
        functools.partial(pack_kernel, group),
        out_shape=[jax.ShapeDtypeStruct((3, rows, HD), query.dtype)] * group,
        in_specs=[VMEM] * 3,
        out_specs=[VMEM] * group,
        compiler_params=PARAMS,
        cost_estimate=pl.CostEstimate(flops=0, bytes_accessed=6 * query.size * 2, transcendentals=0),
    )(query, key, value)


def unpack_kernel(group, *refs):
    out = refs[group]
    for d in range(group):
        col = pl.ds(pl.multiple_of(head_at(group, -d) * HD, HD), HD)
        out[:, col] = refs[d][...]


def unpack(blocks, group):
    rows = blocks[0].shape[0]
    return pl.pallas_call(
        functools.partial(unpack_kernel, group),
        out_shape=jax.ShapeDtypeStruct((rows, group * HD), blocks[0].dtype),
        in_specs=[VMEM] * group,
        out_specs=VMEM,
        compiler_params=PARAMS,
        cost_estimate=pl.CostEstimate(flops=0, bytes_accessed=4 * rows * group * HD, transcendentals=0),
    )(*blocks)


def attention_kernel(group, rows, with_prev, *refs):
    sets = 2 if with_prev else 1
    outs = refs[sets * group : (sets + 1) * group]
    q_s, k_s, v_s, o_s = refs[(sets + 1) * group :]
    base = group * rows if with_prev else 0
    for d in range(group):
        at = head_at(group, -d) * rows
        src = refs[d]
        q_s[pl.ds(pl.multiple_of(at, rows), rows), :] = src[0]
        k_s[pl.ds(pl.multiple_of(base + at, rows), rows), :] = src[1]
        v_s[pl.ds(pl.multiple_of(base + at, rows), rows), :] = src[2]
        if with_prev:
            old = refs[group + d]
            k_s[pl.ds(pl.multiple_of(at, rows), rows), :] = old[0]
            v_s[pl.ds(pl.multiple_of(at, rows), rows), :] = old[1]
    row = lax.broadcasted_iota(jnp.int32, (rows, rows), 0)
    col = lax.broadcasted_iota(jnp.int32, (rows, rows), 1)
    factor = HD**-0.5 * LOG2E
    for i in range(group):
        lo = i * rows if with_prev else 0
        hi = base + (i + 1) * rows
        q = q_s[i * rows : (i + 1) * rows, :]
        s = lax.dot_general(
            q, k_s[lo:hi, :], (((1,), (1,)), ((), ())), preferred_element_type=jnp.float32
        )
        last = jnp.where(col <= row, s[:, hi - lo - rows :], -jnp.inf)
        parts = [s[:, : hi - lo - rows], last] if hi - lo > rows else [last]
        if with_prev:
            held = lax.axis_index("ctx") >= group
            middle = s[:, rows : hi - lo - rows]
            first = jnp.where((col > row) & held, s[:, :rows], -jnp.inf)
            number = lax.broadcasted_iota(jnp.int32, middle.shape, 1) + (lo + rows)
            middle = jnp.where((number >= base) | held, middle, -jnp.inf)
            parts = [first, middle, last]
        s = jnp.concatenate(parts, axis=1) if len(parts) > 1 else parts[0]
        top = jnp.max(s, axis=1, keepdims=True)
        p = jnp.exp2((s - top) * factor)
        total = jnp.sum(p, axis=1, keepdims=True)
        o = jnp.dot(p.astype(jnp.bfloat16), v_s[lo:hi, :], preferred_element_type=jnp.float32)
        o_s[i * rows : (i + 1) * rows, :] = (o / total).astype(jnp.bfloat16)
    for d in range(group):
        at = head_at(group, d) * rows
        outs[d][...] = o_s[pl.ds(pl.multiple_of(at, rows), rows), :]


def attention(blocks, old, group):
    rows = blocks[0].shape[1]
    with_prev = old is not None
    length = group * rows
    keys = length * (2 if with_prev else 1)
    operands = list(blocks) + (list(old) if with_prev else [])
    bf16 = jnp.bfloat16
    return pl.pallas_call(
        functools.partial(attention_kernel, group, rows, with_prev),
        out_shape=[jax.ShapeDtypeStruct((rows, HD), bf16)] * group,
        in_specs=[VMEM] * len(operands),
        out_specs=[VMEM] * group,
        scratch_shapes=[
            pltpu.VMEM((length, HD), bf16),
            pltpu.VMEM((keys, HD), bf16),
            pltpu.VMEM((keys, HD), bf16),
            pltpu.VMEM((length, HD), bf16),
        ],
        compiler_params=PARAMS,
        cost_estimate=pl.CostEstimate(
            flops=2 * length * keys * HD,
            bytes_accessed=8 * length * HD,
            transcendentals=length * keys // 2,
        ),
    )(*operands)


def scan_kernel(delta_ref, x_ref, a_ref, bc_ref, y_ref, d_ref, end_ref, u_s):
    rows = delta_ref.shape[0]
    for c in range(SUB):
        cols = slice(c * LANES, (c + 1) * LANES)
        dt = delta_ref[:, cols]
        d_ref[pl.ds(c, rows, stride=SUB), :] = dt
        u_s[pl.ds(c, rows, stride=SUB), :] = dt * x_ref[:, cols].astype(jnp.float32)

    per = 4

    def step(block, carry):
        states, through = list(carry[:NS]), carry[NS]
        for k in range(per):
            t = block * per + k
            at = pl.ds(pl.multiple_of(t * SUB, SUB), SUB)
            dt, u = d_ref[at, :], u_s[at, :]
            through = through + dt
            sums = [None] * 4
            for n in range(NS):
                e = jnp.exp2(dt * a_ref[n * SUB : (n + 1) * SUB, :])
                states[n] = e * states[n] + u * bc_ref[t, n]
                term = states[n] * bc_ref[t, NS + n]
                sums[n % 4] = term if n < 4 else sums[n % 4] + term
            y_ref[at, :] = (sums[0] + sums[1]) + (sums[2] + sums[3])
        return (*states, through)

    zero = jnp.zeros((SUB, LANES), jnp.float32)
    ends = lax.fori_loop(0, rows // per, step, (zero,) * (NS + 1))
    for n in range(NS + 1):
        end_ref[n * SUB : (n + 1) * SUB, :] = ends[n]


def scan_block(delta, x, rate2, bc):
    rows, channels = delta.shape
    f32 = jnp.float32
    tiles = jax.ShapeDtypeStruct((rows * SUB, LANES), f32)
    return pl.pallas_call(
        scan_kernel,
        out_shape=[tiles, tiles, jax.ShapeDtypeStruct(((NS + 1) * SUB, LANES), f32)],
        in_specs=[VMEM, VMEM, VMEM, SMEM],
        out_specs=[VMEM] * 3,
        scratch_shapes=[pltpu.VMEM((rows * SUB, LANES), f32)],
        compiler_params=PARAMS,
        cost_estimate=pl.CostEstimate(
            flops=200 * rows * channels * NS,
            bytes_accessed=14 * rows * channels,
            transcendentals=rows * channels * NS,
        ),
    )(delta, x, rate2, bc)


def finish_kernel(count, *refs):
    ends = refs[:count]
    y_ref, d_ref, a_ref, bc_ref, x_ref, gate_ref, skip_ref, out_ref, y_s = refs[count:]
    rows = x_ref.shape[0]
    tile = [slice(n * SUB, (n + 1) * SUB) for n in range(NS + 1)]
    states = [jnp.zeros((SUB, LANES), jnp.float32)] * NS
    for end in ends:
        through = end[tile[NS], :]
        states = [
            jnp.exp2(through * a_ref[tile[n], :]) * states[n] + end[tile[n], :] for n in range(NS)
        ]
    per = 4

    def step(block, carry):
        held = list(carry)
        for k in range(per):
            t = block * per + k
            at = pl.ds(pl.multiple_of(t * SUB, SUB), SUB)
            dt = d_ref[at, :]
            sums = [y_ref[at, :], None, None, None]
            for n in range(NS):
                held[n] = jnp.exp2(dt * a_ref[tile[n], :]) * held[n]
                term = held[n] * bc_ref[t, NS + n]
                sums[n % 4] = term if sums[n % 4] is None else sums[n % 4] + term
            y_s[at, :] = (sums[0] + sums[1]) + (sums[2] + sums[3])
        return tuple(held)

    lax.fori_loop(0, rows // per, step, tuple(states))
    for c in range(SUB):
        cols = slice(c * LANES, (c + 1) * LANES)
        y = y_s[pl.ds(c, rows, stride=SUB), :] + skip_ref[:, cols] * x_ref[:, cols].astype(jnp.float32)
        g = gate_ref[:, cols].astype(jnp.float32)
        out_ref[:, cols] = (y * (g / (1.0 + jnp.exp(-g)))).astype(out_ref.dtype)


def finish(ends, y, d, rate2, bc, x, gate, skip):
    rows, channels = x.shape
    return pl.pallas_call(
        functools.partial(finish_kernel, len(ends)),
        out_shape=jax.ShapeDtypeStruct((rows, channels), jnp.bfloat16),
        in_specs=[VMEM] * len(ends) + [VMEM, VMEM, VMEM, SMEM, VMEM, VMEM, VMEM],
        out_specs=VMEM,
        scratch_shapes=[pltpu.VMEM((rows * SUB, LANES), jnp.float32)],
        compiler_params=PARAMS,
        cost_estimate=pl.CostEstimate(
            flops=150 * rows * channels * NS,
            bytes_accessed=14 * rows * channels,
            transcendentals=rows * channels * NS,
        ),
    )(*ends, y, d, rate2, bc, x, gate, skip)


def joined(later, earlier, rate2):
    cut = NS * SUB
    through = jnp.tile(later[cut:], (NS, 1))
    state = jnp.exp2(through * rate2) * earlier[:cut] + later[:cut]
    return jnp.concatenate([state, later[cut:] + earlier[cut:]], axis=0)


def earlier_ends(end, rate2):
    peers = lax.axis_size("ctx")
    if peers <= RADIX:
        return [shifted(end, "ctx", d) for d in range(peers - 1, 0, -1)]
    whole, span = end, 1
    while span < peers:
        away = [d * span for d in range(1, RADIX) if d * span < peers]
        parts = [shifted(whole, "ctx", d) for d in away]
        for part in parts:
            whole = joined(whole, part, rate2)
        span *= RADIX
    return [shifted(whole, "ctx", 1)]


def shards(query, key, value, xin, gate_z, w_bc, dt_low, dt_proj, dt_bias, a_rate, skip):
    rows, channels = xin.shape
    group = query.shape[1] // HD
    assert group * rows == WINDOW and lax.axis_size("ctx") % group == 0
    assert channels == SUB * LANES
    packed = pack(query, key, value, group)
    partial_bc = jnp.dot(xin, w_bc, preferred_element_type=jnp.float32)
    tp = lax.axis_size("tp")
    others = [rotated(partial_bc, "tp", tp, d) for d in range(1, tp)]
    moved = [packed[0]] + [rotated(packed[d], "ctx", group, d) for d in range(1, group)]
    delta = jax.nn.softplus(
        jnp.dot(dt_low, dt_proj, preferred_element_type=jnp.float32) + dt_bias[None, :]
    )
    rate2 = (a_rate * -LOG2E).reshape(NS * SUB, LANES)
    bc = sum(others, partial_bc)
    y, d, end = scan_block(delta, xin, rate2, bc)
    ends = earlier_ends(end, rate2)
    old = None
    if lax.axis_size("ctx") > group:
        old = [shifted(block[1:], "ctx", group) for block in moved]
    outs = attention(moved, old, group)
    back = [outs[0]] + [rotated(outs[d], "ctx", group, d) for d in range(1, group)]
    mixed = finish(ends, y, d, rate2, bc, xin, gate_z, skip[None, :])
    return unpack(back, group), mixed


def solution(mesh):
    two = P("ctx", "tp")
    in_specs = (
        two,
        two,
        two,
        two,
        two,
        P("tp", None),
        P("ctx", None),
        P(None, "tp"),
        P("tp"),
        P(None, "tp"),
        P("tp"),
    )
    return jax.shard_map(
        shards, mesh=mesh, in_specs=in_specs, out_specs=(two, two), check_vma=False
    )
```

```python
import functools
import math

import jax
import jax.numpy as jnp
from jax import lax
from jax.experimental import pallas as pl
from jax.experimental.pallas import tpu as pltpu
from jax.sharding import PartitionSpec as P

HD = 128
WINDOW = 2048
NS = 16
LANES = 128
SUB = 8
LOG2E = math.log2(math.e)
RADIX = 8
VMEM = pl.BlockSpec(memory_space=pltpu.VMEM)
SMEM = pl.BlockSpec(memory_space=pltpu.SMEM)
PARAMS = pltpu.CompilerParams(vmem_limit_bytes=40 * 1024 * 1024)


def shifted(block, axis, distance):
    peers = lax.axis_size(axis)
    return lax.ppermute(block, axis, [(i, i + distance) for i in range(peers - distance)])


def rotated(block, axis, group, distance):
    peers = lax.axis_size(axis)
    route = [(i, i // group * group + (i % group + distance) % group) for i in range(peers)]
    return lax.ppermute(block, axis, route)


def head_at(group, distance):
    slot = lax.rem(lax.axis_index("ctx"), group)
    return lax.rem(slot + distance + group, group)


def pack_kernel(group, q_ref, k_ref, v_ref, *outs):
    for d in range(group):
        col = pl.ds(pl.multiple_of(head_at(group, d) * HD, HD), HD)
        for part, ref in enumerate((q_ref, k_ref, v_ref)):
            outs[d][part] = ref[:, col]


def pack(query, key, value, group):
    rows = query.shape[0]
    return pl.pallas_call(
        functools.partial(pack_kernel, group),
        out_shape=[jax.ShapeDtypeStruct((3, rows, HD), query.dtype)] * group,
        in_specs=[VMEM] * 3,
        out_specs=[VMEM] * group,
        compiler_params=PARAMS,
        cost_estimate=pl.CostEstimate(flops=0, bytes_accessed=6 * query.size * 2, transcendentals=0),
    )(query, key, value)


def unpack_kernel(group, *refs):
    out = refs[group]
    for d in range(group):
        col = pl.ds(pl.multiple_of(head_at(group, -d) * HD, HD), HD)
        out[:, col] = refs[d][...]


def unpack(blocks, group):
    rows = blocks[0].shape[0]
    return pl.pallas_call(
        functools.partial(unpack_kernel, group),
        out_shape=jax.ShapeDtypeStruct((rows, group * HD), blocks[0].dtype),
        in_specs=[VMEM] * group,
        out_specs=VMEM,
        compiler_params=PARAMS,
        cost_estimate=pl.CostEstimate(flops=0, bytes_accessed=4 * rows * group * HD, transcendentals=0),
    )(*blocks)


def attention_kernel(group, rows, with_prev, *refs):
    sets = 2 if with_prev else 1
    outs = refs[sets * group : (sets + 1) * group]
    q_s, k_s, v_s, o_s = refs[(sets + 1) * group :]
    base = group * rows if with_prev else 0
    for d in range(group):
        at = head_at(group, -d) * rows
        src = refs[d]
        q_s[pl.ds(pl.multiple_of(at, rows), rows), :] = src[0]
        k_s[pl.ds(pl.multiple_of(base + at, rows), rows), :] = src[1]
        v_s[pl.ds(pl.multiple_of(base + at, rows), rows), :] = src[2]
        if with_prev:
            old = refs[group + d]
            k_s[pl.ds(pl.multiple_of(at, rows), rows), :] = old[0]
            v_s[pl.ds(pl.multiple_of(at, rows), rows), :] = old[1]
    row = lax.broadcasted_iota(jnp.int32, (rows, rows), 0)
    col = lax.broadcasted_iota(jnp.int32, (rows, rows), 1)
    factor = HD**-0.5 * LOG2E
    for i in range(group):
        lo = i * rows if with_prev else 0
        hi = base + (i + 1) * rows
        q = q_s[i * rows : (i + 1) * rows, :]
        s = lax.dot_general(
            q, k_s[lo:hi, :], (((1,), (1,)), ((), ())), preferred_element_type=jnp.float32
        )
        last = jnp.where(col <= row, s[:, hi - lo - rows :], -jnp.inf)
        parts = [s[:, : hi - lo - rows], last] if hi - lo > rows else [last]
        if with_prev:
            held = lax.axis_index("ctx") >= group
            middle = s[:, rows : hi - lo - rows]
            first = jnp.where((col > row) & held, s[:, :rows], -jnp.inf)
            number = lax.broadcasted_iota(jnp.int32, middle.shape, 1) + (lo + rows)
            middle = jnp.where((number >= base) | held, middle, -jnp.inf)
            parts = [first, middle, last]
        s = jnp.concatenate(parts, axis=1) if len(parts) > 1 else parts[0]
        top = jnp.max(s, axis=1, keepdims=True)
        p = jnp.exp2((s - top) * factor)
        total = jnp.sum(p, axis=1, keepdims=True)
        o = jnp.dot(p.astype(jnp.bfloat16), v_s[lo:hi, :], preferred_element_type=jnp.float32)
        o_s[i * rows : (i + 1) * rows, :] = (o / total).astype(jnp.bfloat16)
    for d in range(group):
        at = head_at(group, d) * rows
        outs[d][...] = o_s[pl.ds(pl.multiple_of(at, rows), rows), :]


def attention(blocks, old, group):
    rows = blocks[0].shape[1]
    with_prev = old is not None
    length = group * rows
    keys = length * (2 if with_prev else 1)
    operands = list(blocks) + (list(old) if with_prev else [])
    bf16 = jnp.bfloat16
    return pl.pallas_call(
        functools.partial(attention_kernel, group, rows, with_prev),
        out_shape=[jax.ShapeDtypeStruct((rows, HD), bf16)] * group,
        in_specs=[VMEM] * len(operands),
        out_specs=[VMEM] * group,
        scratch_shapes=[
            pltpu.VMEM((length, HD), bf16),
            pltpu.VMEM((keys, HD), bf16),
            pltpu.VMEM((keys, HD), bf16),
            pltpu.VMEM((length, HD), bf16),
        ],
        compiler_params=PARAMS,
        cost_estimate=pl.CostEstimate(
            flops=2 * length * keys * HD,
            bytes_accessed=8 * length * HD,
            transcendentals=length * keys // 2,
        ),
    )(*operands)


def scan_kernel(delta_ref, x_ref, a_ref, bc_ref, y_ref, d_ref, end_ref, u_s):
    rows = delta_ref.shape[0]
    for c in range(SUB):
        cols = slice(c * LANES, (c + 1) * LANES)
        dt = delta_ref[:, cols]
        d_ref[pl.ds(c, rows, stride=SUB), :] = dt
        u_s[pl.ds(c, rows, stride=SUB), :] = dt * x_ref[:, cols].astype(jnp.float32)

    per = 4

    def step(block, carry):
        states, through = list(carry[:NS]), carry[NS]
        for k in range(per):
            t = block * per + k
            at = pl.ds(pl.multiple_of(t * SUB, SUB), SUB)
            dt, u = d_ref[at, :], u_s[at, :]
            through = through + dt
            sums = [None] * 4
            for n in range(NS):
                e = jnp.exp2(dt * a_ref[n * SUB : (n + 1) * SUB, :])
                states[n] = e * states[n] + u * bc_ref[t, n]
                term = states[n] * bc_ref[t, NS + n]
                sums[n % 4] = term if n < 4 else sums[n % 4] + term
            y_ref[at, :] = (sums[0] + sums[1]) + (sums[2] + sums[3])
        return (*states, through)

    zero = jnp.zeros((SUB, LANES), jnp.float32)
    ends = lax.fori_loop(0, rows // per, step, (zero,) * (NS + 1))
    for n in range(NS + 1):
        end_ref[n * SUB : (n + 1) * SUB, :] = ends[n]


def scan_block(delta, x, rate2, bc):
    rows, channels = delta.shape
    f32 = jnp.float32
    tiles = jax.ShapeDtypeStruct((rows * SUB, LANES), f32)
    return pl.pallas_call(
        scan_kernel,
        out_shape=[tiles, tiles, jax.ShapeDtypeStruct(((NS + 1) * SUB, LANES), f32)],
        in_specs=[VMEM, VMEM, VMEM, SMEM],
        out_specs=[VMEM] * 3,
        scratch_shapes=[pltpu.VMEM((rows * SUB, LANES), f32)],
        compiler_params=PARAMS,
        cost_estimate=pl.CostEstimate(
            flops=200 * rows * channels * NS,
            bytes_accessed=14 * rows * channels,
            transcendentals=rows * channels * NS,
        ),
    )(delta, x, rate2, bc)


def finish_kernel(count, *refs):
    ends = refs[:count]
    y_ref, d_ref, a_ref, bc_ref, x_ref, gate_ref, skip_ref, out_ref, y_s = refs[count:]
    rows = x_ref.shape[0]
    tile = [slice(n * SUB, (n + 1) * SUB) for n in range(NS + 1)]
    states = [jnp.zeros((SUB, LANES), jnp.float32)] * NS
    for end in ends:
        through = end[tile[NS], :]
        states = [
            jnp.exp2(through * a_ref[tile[n], :]) * states[n] + end[tile[n], :] for n in range(NS)
        ]
    per = 4

    def step(block, carry):
        held = list(carry)
        for k in range(per):
            t = block * per + k
            at = pl.ds(pl.multiple_of(t * SUB, SUB), SUB)
            dt = d_ref[at, :]
            sums = [y_ref[at, :], None, None, None]
            for n in range(NS):
                held[n] = jnp.exp2(dt * a_ref[tile[n], :]) * held[n]
                term = held[n] * bc_ref[t, NS + n]
                sums[n % 4] = term if sums[n % 4] is None else sums[n % 4] + term
            y_s[at, :] = (sums[0] + sums[1]) + (sums[2] + sums[3])
        return tuple(held)

    lax.fori_loop(0, rows // per, step, tuple(states))
    for c in range(SUB):
        cols = slice(c * LANES, (c + 1) * LANES)
        y = y_s[pl.ds(c, rows, stride=SUB), :] + skip_ref[:, cols] * x_ref[:, cols].astype(jnp.float32)
        g = gate_ref[:, cols].astype(jnp.float32)
        out_ref[:, cols] = (y * (g / (1.0 + jnp.exp(-g)))).astype(out_ref.dtype)


def finish(ends, y, d, rate2, bc, x, gate, skip):
    rows, channels = x.shape
    return pl.pallas_call(
        functools.partial(finish_kernel, len(ends)),
        out_shape=jax.ShapeDtypeStruct((rows, channels), jnp.bfloat16),
        in_specs=[VMEM] * len(ends) + [VMEM, VMEM, VMEM, SMEM, VMEM, VMEM, VMEM],
        out_specs=VMEM,
        scratch_shapes=[pltpu.VMEM((rows * SUB, LANES), jnp.float32)],
        compiler_params=PARAMS,
        cost_estimate=pl.CostEstimate(
            flops=150 * rows * channels * NS,
            bytes_accessed=14 * rows * channels,
            transcendentals=rows * channels * NS,
        ),
    )(*ends, y, d, rate2, bc, x, gate, skip)


def joined(later, earlier, rate2):
    cut = NS * SUB
    through = jnp.tile(later[cut:], (NS, 1))
    state = jnp.exp2(through * rate2) * earlier[:cut] + later[:cut]
    return jnp.concatenate([state, later[cut:] + earlier[cut:]], axis=0)


def earlier_ends(end, rate2):
    peers = lax.axis_size("ctx")
    whole, span = end, 1
    while span < peers:
        away = [d * span for d in range(1, RADIX) if d * span < peers]
        parts = [shifted(whole, "ctx", d) for d in away]
        for part in parts:
            whole = joined(whole, part, rate2)
        span *= RADIX
    return [shifted(whole, "ctx", 1)]


def send(src, dst, sems, at, axis, peer):
    return pltpu.make_async_remote_copy(
        src_ref=src,
        dst_ref=dst,
        send_sem=sems.at[0, at],
        recv_sem=sems.at[1, at],
        device_id={axis: peer},
        device_id_type=pl.DeviceIdType.MESH,
    )


def whole_kernel(group, tp, *refs):
    q_ref, k_ref, v_ref, x_ref, gate_ref, delta_ref, part_ref, a_ref, skip_ref = refs[:9]
    att_ref, mix_ref = refs[9:11]
    (pack_s, got_s, bcs_s, bc_v, bc_s, y_s, d_s, u_s, end_s, ends_s, inc_s, o_s, back_s) = refs[11:24]
    bc_sem, qkv_sem, end_sem, out_sem, copy_sem = refs[24:]
    rows = x_ref.shape[0]
    slot = lax.axis_index("ctx")
    line = lax.axis_index("tp")
    peer = [lax.rem(slot + d, group) for d in range(group)]
    origin = [lax.rem(slot - d + group, group) for d in range(group)]

    barrier = pltpu.get_barrier_semaphore()
    for d in range(1, group):
        pl.semaphore_signal(
            barrier, inc=1, device_id={"ctx": peer[d]}, device_id_type=pl.DeviceIdType.MESH
        )
    for d in range(1, tp):
        pl.semaphore_signal(
            barrier,
            inc=1,
            device_id={"tp": lax.rem(line + d, tp)},
            device_id_type=pl.DeviceIdType.MESH,
        )
    for d in range(1, group):
        col = pl.ds(pl.multiple_of(peer[d] * HD, HD), HD)
        for part, ref in enumerate((q_ref, k_ref, v_ref)):
            pack_s[d - 1, part] = ref[:, col]
    col = pl.ds(pl.multiple_of(slot * HD, HD), HD)
    for part, ref in enumerate((q_ref, k_ref, v_ref)):
        got_s[slot, part] = ref[:, col]
    pl.semaphore_wait(barrier, group + tp - 2)

    bc_copies = [
        send(part_ref, bcs_s.at[d - 1], bc_sem, d - 1, "tp", lax.rem(line + d, tp))
        for d in range(1, tp)
    ]
    for copy in bc_copies:
        copy.start()
    qkv_copies = [
        send(pack_s.at[d - 1], got_s.at[slot], qkv_sem, d - 1, "ctx", peer[d])
        for d in range(1, group)
    ]
    for copy in qkv_copies:
        copy.start()

    for c in range(SUB):
        cols = slice(c * LANES, (c + 1) * LANES)
        dt = delta_ref[:, cols]
        d_s[pl.ds(c, rows, stride=SUB), :] = dt
        u_s[pl.ds(c, rows, stride=SUB), :] = dt * x_ref[:, cols].astype(jnp.float32)
    total = part_ref[...]
    for d in range(1, tp):
        bc_copies[d - 1].wait()
        total = total + bcs_s[d - 1]
    bc_v[...] = total
    to_scalars = pltpu.make_async_copy(bc_v, bc_s, copy_sem)
    to_scalars.start()
    to_scalars.wait()

    tile = [slice(n * SUB, (n + 1) * SUB) for n in range(NS + 1)]
    per = 4

    def step(block, carry):
        states, through = list(carry[:NS]), carry[NS]
        for k in range(per):
            t = block * per + k
            at = pl.ds(pl.multiple_of(t * SUB, SUB), SUB)
            dt, u = d_s[at, :], u_s[at, :]
            through = through + dt
            sums = [None] * 4
            for n in range(NS):
                e = jnp.exp2(dt * a_ref[tile[n], :])
                states[n] = e * states[n] + u * bc_s[n, t]
                term = states[n] * bc_s[NS + n, t]
                sums[n % 4] = term if n < 4 else sums[n % 4] + term
            y_s[at, :] = (sums[0] + sums[1]) + (sums[2] + sums[3])
        return (*states, through)

    zero = jnp.zeros((SUB, LANES), jnp.float32)
    ends = lax.fori_loop(0, rows // per, step, (zero,) * (NS + 1))
    for n in range(NS + 1):
        end_s[tile[n], :] = ends[n]

    end_copies = [
        send(end_s, ends_s.at[d - 1], end_sem, d - 1, "ctx", peer[d]) for d in range(1, group)
    ]
    for d in range(1, group):
        pl.when(slot + d < group)(end_copies[d - 1].start)

    for copy in qkv_copies:
        copy.wait()
    row = lax.broadcasted_iota(jnp.int32, (rows, rows), 0)
    col = lax.broadcasted_iota(jnp.int32, (rows, rows), 1)
    factor = HD**-0.5 * LOG2E
    for i in range(group):
        q = got_s[i, 0]
        keys = got_s[: i + 1, 1].reshape((i + 1) * rows, HD)
        values = got_s[: i + 1, 2].reshape((i + 1) * rows, HD)
        s = lax.dot_general(
            q, keys, (((1,), (1,)), ((), ())), preferred_element_type=jnp.float32
        )
        last = jnp.where(col <= row, s[:, i * rows :], -jnp.inf)
        s = jnp.concatenate([s[:, : i * rows], last], axis=1) if i else last
        top = jnp.max(s, axis=1, keepdims=True)
        p = jnp.exp2((s - top) * factor)
        o = jnp.dot(p.astype(jnp.bfloat16), values, preferred_element_type=jnp.float32)
        o_s[i] = (o / jnp.sum(p, axis=1, keepdims=True)).astype(jnp.bfloat16)

    out_copies = [
        send(o_s.at[peer[d]], back_s.at[d - 1], out_sem, d - 1, "ctx", peer[d])
        for d in range(1, group)
    ]
    for copy in out_copies:
        copy.start()

    inc_s[...] = jnp.zeros_like(inc_s)
    for d in range(group - 1, 0, -1):

        @pl.when(slot >= d)
        def _(d=d):
            end_copies[d - 1].wait_recv()
            through = ends_s[d - 1, tile[NS], :]
            for n in range(NS):
                inc_s[tile[n], :] = (
                    jnp.exp2(through * a_ref[tile[n], :]) * inc_s[tile[n], :]
                    + ends_s[d - 1, tile[n], :]
                )

    def correct(block, carry):
        held = list(carry)
        for k in range(per):
            t = block * per + k
            at = pl.ds(pl.multiple_of(t * SUB, SUB), SUB)
            dt = d_s[at, :]
            sums = [y_s[at, :], None, None, None]
            for n in range(NS):
                held[n] = jnp.exp2(dt * a_ref[tile[n], :]) * held[n]
                term = held[n] * bc_s[NS + n, t]
                sums[n % 4] = term if sums[n % 4] is None else sums[n % 4] + term
            y_s[at, :] = (sums[0] + sums[1]) + (sums[2] + sums[3])
        return tuple(held)

    lax.fori_loop(0, rows // per, correct, tuple(inc_s[tile[n], :] for n in range(NS)))
    for c in range(SUB):
        cols = slice(c * LANES, (c + 1) * LANES)
        y = y_s[pl.ds(c, rows, stride=SUB), :] + skip_ref[:, cols] * x_ref[:, cols].astype(jnp.float32)
        g = gate_ref[:, cols].astype(jnp.float32)
        mix_ref[:, cols] = (y * (g / (1.0 + jnp.exp(-g)))).astype(mix_ref.dtype)

    att_ref[:, pl.ds(pl.multiple_of(slot * HD, HD), HD)] = o_s[slot]
    for d in range(1, group):
        out_copies[d - 1].wait()
        att_ref[:, pl.ds(pl.multiple_of(origin[d] * HD, HD), HD)] = back_s[d - 1]
    for d in range(1, group):
        pl.when(slot + d < group)(end_copies[d - 1].wait_send)


def whole(query, key, value, xin, gate_z, delta, part, rate2, skip):
    rows, channels = xin.shape
    group, tp = lax.axis_size("ctx"), lax.axis_size("tp")
    f32, bf16 = jnp.float32, jnp.bfloat16
    tiles = pltpu.VMEM((rows * SUB, LANES), f32)
    ends = ((NS + 1) * SUB, LANES)
    return pl.pallas_call(
        functools.partial(whole_kernel, group, tp),
        out_shape=[jax.ShapeDtypeStruct((rows, channels), bf16)] * 2,
        in_specs=[VMEM] * 9,
        out_specs=[VMEM] * 2,
        scratch_shapes=[
            pltpu.VMEM((group - 1, 3, rows, HD), bf16),
            pltpu.VMEM((group, 3, rows, HD), bf16),
            pltpu.VMEM((tp - 1, 2 * NS, rows), f32),
            pltpu.VMEM((2 * NS, rows), f32),
            pltpu.SMEM((2 * NS, rows), f32),
            tiles,
            tiles,
            tiles,
            pltpu.VMEM(ends, f32),
            pltpu.VMEM((group - 1, *ends), f32),
            pltpu.VMEM((NS * SUB, LANES), f32),
            pltpu.VMEM((group, rows, HD), bf16),
            pltpu.VMEM((group - 1, rows, HD), bf16),
            pltpu.SemaphoreType.DMA((2, tp - 1)),
            pltpu.SemaphoreType.DMA((2, group - 1)),
            pltpu.SemaphoreType.DMA((2, group - 1)),
            pltpu.SemaphoreType.DMA((2, group - 1)),
            pltpu.SemaphoreType.DMA,
        ],
        compiler_params=pltpu.CompilerParams(
            collective_id=0, has_side_effects=True, vmem_limit_bytes=40 * 1024 * 1024
        ),
    )(query, key, value, xin, gate_z, delta, part, rate2, skip)


def shards(query, key, value, xin, gate_z, w_bc, dt_low, dt_proj, dt_bias, a_rate, skip):
    rows, channels = xin.shape
    group = query.shape[1] // HD
    assert group * rows == WINDOW and lax.axis_size("ctx") % group == 0
    assert channels == SUB * LANES
    delta = jax.nn.softplus(
        jnp.dot(dt_low, dt_proj, preferred_element_type=jnp.float32) + dt_bias[None, :]
    )
    rate2 = (a_rate * -LOG2E).reshape(NS * SUB, LANES)
    if lax.axis_size("ctx") == group:
        part = lax.dot_general(
            w_bc, xin, (((0,), (1,)), ((), ())), preferred_element_type=jnp.float32
        )
        return tuple(whole(query, key, value, xin, gate_z, delta, part, rate2, skip[None, :]))
    packed = pack(query, key, value, group)
    partial_bc = jnp.dot(xin, w_bc, preferred_element_type=jnp.float32)
    tp = lax.axis_size("tp")
    others = [rotated(partial_bc, "tp", tp, d) for d in range(1, tp)]
    moved = [packed[0]] + [rotated(packed[d], "ctx", group, d) for d in range(1, group)]
    bc = sum(others, partial_bc)
    y, d, end = scan_block(delta, xin, rate2, bc)
    ends = earlier_ends(end, rate2)
    old = [shifted(block[1:], "ctx", group) for block in moved]
    outs = attention(moved, old, group)
    back = [outs[0]] + [rotated(outs[d], "ctx", group, d) for d in range(1, group)]
    mixed = finish(ends, y, d, rate2, bc, xin, gate_z, skip[None, :])
    return unpack(back, group), mixed


def solution(mesh):
    two = P("ctx", "tp")
    in_specs = (
        two,
        two,
        two,
        two,
        two,
        P("tp", None),
        P("ctx", None),
        P(None, "tp"),
        P("tp"),
        P(None, "tp"),
        P("tp"),
    )
    return jax.shard_map(
        shards, mesh=mesh, in_specs=in_specs, out_specs=(two, two), check_vma=False
    )
```

```python
import functools
import math

import jax
import jax.numpy as jnp
from jax import lax
from jax.experimental import pallas as pl
from jax.experimental.pallas import tpu as pltpu
from jax.sharding import PartitionSpec as P

HD = 128
WINDOW = 2048
NS = 16
LANES = 128
SUB = 8
LOG2E = math.log2(math.e)
RADIX = 8
VMEM = pl.BlockSpec(memory_space=pltpu.VMEM)
SMEM = pl.BlockSpec(memory_space=pltpu.SMEM)
PARAMS = pltpu.CompilerParams(vmem_limit_bytes=40 * 1024 * 1024)


def shifted(block, axis, distance):
    peers = lax.axis_size(axis)
    return lax.ppermute(block, axis, [(i, i + distance) for i in range(peers - distance)])


def rotated(block, axis, group, distance):
    peers = lax.axis_size(axis)
    route = [(i, i // group * group + (i % group + distance) % group) for i in range(peers)]
    return lax.ppermute(block, axis, route)


def head_at(group, distance):
    slot = lax.rem(lax.axis_index("ctx"), group)
    return lax.rem(slot + distance + group, group)


def pack_kernel(group, q_ref, k_ref, v_ref, *outs):
    for d in range(group):
        col = pl.ds(pl.multiple_of(head_at(group, d) * HD, HD), HD)
        for part, ref in enumerate((q_ref, k_ref, v_ref)):
            outs[d][part] = ref[:, col]


def pack(query, key, value, group):
    rows = query.shape[0]
    return pl.pallas_call(
        functools.partial(pack_kernel, group),
        out_shape=[jax.ShapeDtypeStruct((3, rows, HD), query.dtype)] * group,
        in_specs=[VMEM] * 3,
        out_specs=[VMEM] * group,
        compiler_params=PARAMS,
        cost_estimate=pl.CostEstimate(flops=0, bytes_accessed=6 * query.size * 2, transcendentals=0),
    )(query, key, value)


def unpack_kernel(group, *refs):
    out = refs[group]
    for d in range(group):
        col = pl.ds(pl.multiple_of(head_at(group, -d) * HD, HD), HD)
        out[:, col] = refs[d][...]


def unpack(blocks, group):
    rows = blocks[0].shape[0]
    return pl.pallas_call(
        functools.partial(unpack_kernel, group),
        out_shape=jax.ShapeDtypeStruct((rows, group * HD), blocks[0].dtype),
        in_specs=[VMEM] * group,
        out_specs=VMEM,
        compiler_params=PARAMS,
        cost_estimate=pl.CostEstimate(flops=0, bytes_accessed=4 * rows * group * HD, transcendentals=0),
    )(*blocks)


def attention_kernel(group, rows, with_prev, *refs):
    sets = 2 if with_prev else 1
    outs = refs[sets * group : (sets + 1) * group]
    q_s, k_s, v_s, o_s = refs[(sets + 1) * group :]
    base = group * rows if with_prev else 0
    for d in range(group):
        at = head_at(group, -d) * rows
        src = refs[d]
        q_s[pl.ds(pl.multiple_of(at, rows), rows), :] = src[0]
        k_s[pl.ds(pl.multiple_of(base + at, rows), rows), :] = src[1]
        v_s[pl.ds(pl.multiple_of(base + at, rows), rows), :] = src[2]
        if with_prev:
            old = refs[group + d]
            k_s[pl.ds(pl.multiple_of(at, rows), rows), :] = old[0]
            v_s[pl.ds(pl.multiple_of(at, rows), rows), :] = old[1]
    row = lax.broadcasted_iota(jnp.int32, (rows, rows), 0)
    col = lax.broadcasted_iota(jnp.int32, (rows, rows), 1)
    factor = HD**-0.5 * LOG2E
    for i in range(group):
        lo = i * rows if with_prev else 0
        hi = base + (i + 1) * rows
        q = q_s[i * rows : (i + 1) * rows, :]
        s = lax.dot_general(
            q, k_s[lo:hi, :], (((1,), (1,)), ((), ())), preferred_element_type=jnp.float32
        )
        last = jnp.where(col <= row, s[:, hi - lo - rows :], -jnp.inf)
        parts = [s[:, : hi - lo - rows], last] if hi - lo > rows else [last]
        if with_prev:
            held = lax.axis_index("ctx") >= group
            middle = s[:, rows : hi - lo - rows]
            first = jnp.where((col > row) & held, s[:, :rows], -jnp.inf)
            number = lax.broadcasted_iota(jnp.int32, middle.shape, 1) + (lo + rows)
            middle = jnp.where((number >= base) | held, middle, -jnp.inf)
            parts = [first, middle, last]
        s = jnp.concatenate(parts, axis=1) if len(parts) > 1 else parts[0]
        top = jnp.max(s, axis=1, keepdims=True)
        p = jnp.exp2((s - top) * factor)
        total = jnp.sum(p, axis=1, keepdims=True)
        o = jnp.dot(p.astype(jnp.bfloat16), v_s[lo:hi, :], preferred_element_type=jnp.float32)
        o_s[i * rows : (i + 1) * rows, :] = (o / total).astype(jnp.bfloat16)
    for d in range(group):
        at = head_at(group, d) * rows
        outs[d][...] = o_s[pl.ds(pl.multiple_of(at, rows), rows), :]


def attention(blocks, old, group):
    rows = blocks[0].shape[1]
    with_prev = old is not None
    length = group * rows
    keys = length * (2 if with_prev else 1)
    operands = list(blocks) + (list(old) if with_prev else [])
    bf16 = jnp.bfloat16
    return pl.pallas_call(
        functools.partial(attention_kernel, group, rows, with_prev),
        out_shape=[jax.ShapeDtypeStruct((rows, HD), bf16)] * group,
        in_specs=[VMEM] * len(operands),
        out_specs=[VMEM] * group,
        scratch_shapes=[
            pltpu.VMEM((length, HD), bf16),
            pltpu.VMEM((keys, HD), bf16),
            pltpu.VMEM((keys, HD), bf16),
            pltpu.VMEM((length, HD), bf16),
        ],
        compiler_params=PARAMS,
        cost_estimate=pl.CostEstimate(
            flops=2 * length * keys * HD,
            bytes_accessed=8 * length * HD,
            transcendentals=length * keys // 2,
        ),
    )(*operands)


def scan_kernel(delta_ref, x_ref, a_ref, bc_ref, y_ref, d_ref, end_ref, u_s):
    rows = delta_ref.shape[0]
    for c in range(SUB):
        cols = slice(c * LANES, (c + 1) * LANES)
        dt = delta_ref[:, cols]
        d_ref[pl.ds(c, rows, stride=SUB), :] = dt
        u_s[pl.ds(c, rows, stride=SUB), :] = dt * x_ref[:, cols].astype(jnp.float32)

    per = 4

    def step(block, carry):
        states, through = list(carry[:NS]), carry[NS]
        for k in range(per):
            t = block * per + k
            at = pl.ds(pl.multiple_of(t * SUB, SUB), SUB)
            dt, u = d_ref[at, :], u_s[at, :]
            through = through + dt
            sums = [None] * 4
            for n in range(NS):
                e = jnp.exp2(dt * a_ref[n * SUB : (n + 1) * SUB, :])
                states[n] = e * states[n] + u * bc_ref[t, n]
                term = states[n] * bc_ref[t, NS + n]
                sums[n % 4] = term if n < 4 else sums[n % 4] + term
            y_ref[at, :] = (sums[0] + sums[1]) + (sums[2] + sums[3])
        return (*states, through)

    zero = jnp.zeros((SUB, LANES), jnp.float32)
    ends = lax.fori_loop(0, rows // per, step, (zero,) * (NS + 1))
    for n in range(NS + 1):
        end_ref[n * SUB : (n + 1) * SUB, :] = ends[n]


def scan_block(delta, x, rate2, bc):
    rows, channels = delta.shape
    f32 = jnp.float32
    tiles = jax.ShapeDtypeStruct((rows * SUB, LANES), f32)
    return pl.pallas_call(
        scan_kernel,
        out_shape=[tiles, tiles, jax.ShapeDtypeStruct(((NS + 1) * SUB, LANES), f32)],
        in_specs=[VMEM, VMEM, VMEM, SMEM],
        out_specs=[VMEM] * 3,
        scratch_shapes=[pltpu.VMEM((rows * SUB, LANES), f32)],
        compiler_params=PARAMS,
        cost_estimate=pl.CostEstimate(
            flops=200 * rows * channels * NS,
            bytes_accessed=14 * rows * channels,
            transcendentals=rows * channels * NS,
        ),
    )(delta, x, rate2, bc)


def finish_kernel(count, *refs):
    ends = refs[:count]
    y_ref, d_ref, a_ref, bc_ref, x_ref, gate_ref, skip_ref, out_ref, y_s = refs[count:]
    rows = x_ref.shape[0]
    tile = [slice(n * SUB, (n + 1) * SUB) for n in range(NS + 1)]
    states = [jnp.zeros((SUB, LANES), jnp.float32)] * NS
    for end in ends:
        through = end[tile[NS], :]
        states = [
            jnp.exp2(through * a_ref[tile[n], :]) * states[n] + end[tile[n], :] for n in range(NS)
        ]
    per = 4

    def step(block, carry):
        held = list(carry)
        for k in range(per):
            t = block * per + k
            at = pl.ds(pl.multiple_of(t * SUB, SUB), SUB)
            dt = d_ref[at, :]
            sums = [y_ref[at, :], None, None, None]
            for n in range(NS):
                held[n] = jnp.exp2(dt * a_ref[tile[n], :]) * held[n]
                term = held[n] * bc_ref[t, NS + n]
                sums[n % 4] = term if sums[n % 4] is None else sums[n % 4] + term
            y_s[at, :] = (sums[0] + sums[1]) + (sums[2] + sums[3])
        return tuple(held)

    lax.fori_loop(0, rows // per, step, tuple(states))
    for c in range(SUB):
        cols = slice(c * LANES, (c + 1) * LANES)
        y = y_s[pl.ds(c, rows, stride=SUB), :] + skip_ref[:, cols] * x_ref[:, cols].astype(jnp.float32)
        g = gate_ref[:, cols].astype(jnp.float32)
        out_ref[:, cols] = (y * (g / (1.0 + jnp.exp(-g)))).astype(out_ref.dtype)


def finish(ends, y, d, rate2, bc, x, gate, skip):
    rows, channels = x.shape
    return pl.pallas_call(
        functools.partial(finish_kernel, len(ends)),
        out_shape=jax.ShapeDtypeStruct((rows, channels), jnp.bfloat16),
        in_specs=[VMEM] * len(ends) + [VMEM, VMEM, VMEM, SMEM, VMEM, VMEM, VMEM],
        out_specs=VMEM,
        scratch_shapes=[pltpu.VMEM((rows * SUB, LANES), jnp.float32)],
        compiler_params=PARAMS,
        cost_estimate=pl.CostEstimate(
            flops=150 * rows * channels * NS,
            bytes_accessed=14 * rows * channels,
            transcendentals=rows * channels * NS,
        ),
    )(*ends, y, d, rate2, bc, x, gate, skip)


def joined(later, earlier, rate2):
    cut = NS * SUB
    through = jnp.tile(later[cut:], (NS, 1))
    state = jnp.exp2(through * rate2) * earlier[:cut] + later[:cut]
    return jnp.concatenate([state, later[cut:] + earlier[cut:]], axis=0)


def earlier_ends(end, rate2):
    peers = lax.axis_size("ctx")
    whole, span = end, 1
    while span < peers:
        away = [d * span for d in range(1, RADIX) if d * span < peers]
        parts = [shifted(whole, "ctx", d) for d in away]
        for part in parts:
            whole = joined(whole, part, rate2)
        span *= RADIX
    return [shifted(whole, "ctx", 1)]


def send(src, dst, sems, at, axis, peer):
    return pltpu.make_async_remote_copy(
        src_ref=src,
        dst_ref=dst,
        send_sem=sems.at[0, at],
        recv_sem=sems.at[1, at],
        device_id={axis: peer},
        device_id_type=pl.DeviceIdType.MESH,
    )


def whole_kernel(group, tp, *refs):
    q_ref, k_ref, v_ref, x_ref, gate_ref, delta_ref, part_ref, a_ref, skip_ref = refs[:9]
    att_ref, mix_ref = refs[9:11]
    (pack_s, got_s, bcs_s, bc_v, bc_s, y_s, d_s, u_s, end_s, ends_s, inc_s, all_s, first_s, o_s, back_s) = refs[11:26]
    bc_sem, qkv_sem, end_sem, first_sem, out_sem, copy_sem = refs[26:]
    rows = x_ref.shape[0]
    slot = lax.axis_index("ctx")
    line = lax.axis_index("tp")
    peer = [lax.rem(slot + d, group) for d in range(group)]

    barrier = pltpu.get_barrier_semaphore()
    for d in range(1, group):
        pl.semaphore_signal(
            barrier, inc=1, device_id={"ctx": peer[d]}, device_id_type=pl.DeviceIdType.MESH
        )
    for d in range(1, tp):
        pl.semaphore_signal(
            barrier,
            inc=1,
            device_id={"tp": lax.rem(line + d, tp)},
            device_id_type=pl.DeviceIdType.MESH,
        )
    for d in range(1, group):
        col = pl.ds(pl.multiple_of(peer[d] * HD, HD), HD)
        for part, ref in enumerate((q_ref, k_ref, v_ref)):
            pack_s[d - 1, part] = ref[:, col]
    col = pl.ds(pl.multiple_of(slot * HD, HD), HD)
    for part, ref in enumerate((q_ref, k_ref, v_ref)):
        got_s[slot, part] = ref[:, col]
    pl.semaphore_wait(barrier, group + tp - 2)

    bc_copies = [
        send(part_ref, bcs_s.at[d - 1], bc_sem, d - 1, "tp", lax.rem(line + d, tp))
        for d in range(1, tp)
    ]
    for copy in bc_copies:
        copy.start()
    qkv_copies = [
        send(pack_s.at[d - 1], got_s.at[slot], qkv_sem, d - 1, "ctx", peer[d])
        for d in range(1, group)
    ]
    for copy in qkv_copies:
        copy.start()

    for c in range(SUB):
        cols = slice(c * LANES, (c + 1) * LANES)
        dt = delta_ref[:, cols]
        d_s[pl.ds(c, rows, stride=SUB), :] = dt
        u_s[pl.ds(c, rows, stride=SUB), :] = dt * x_ref[:, cols].astype(jnp.float32)
    total = part_ref[...]
    for d in range(1, tp):
        bc_copies[d - 1].wait()
        total = total + bcs_s[d - 1]
    bc_v[...] = total
    to_scalars = pltpu.make_async_copy(bc_v, bc_s, copy_sem)
    to_scalars.start()
    to_scalars.wait()

    tile = [slice(n * SUB, (n + 1) * SUB) for n in range(NS + 1)]
    per = 4

    def step(block, carry):
        states, through = list(carry[:NS]), carry[NS]
        for k in range(per):
            t = block * per + k
            at = pl.ds(pl.multiple_of(t * SUB, SUB), SUB)
            dt, u = d_s[at, :], u_s[at, :]
            through = through + dt
            sums = [None] * 4
            for n in range(NS):
                e = jnp.exp2(dt * a_ref[tile[n], :])
                states[n] = e * states[n] + u * bc_s[n, t]
                term = states[n] * bc_s[NS + n, t]
                sums[n % 4] = term if n < 4 else sums[n % 4] + term
            y_s[at, :] = (sums[0] + sums[1]) + (sums[2] + sums[3])
        return (*states, through)

    zero = jnp.zeros((SUB, LANES), jnp.float32)
    ends = lax.fori_loop(0, rows // per, step, (zero,) * (NS + 1))
    for n in range(NS + 1):
        end_s[tile[n], :] = ends[n]

    half = group // 2
    place = lax.rem(slot, half)
    end_copies = [
        send(end_s, ends_s.at[d - 1], end_sem, d - 1, "ctx", peer[d]) for d in range(1, half)
    ]
    for d in range(1, half):
        pl.when(place + d < half)(end_copies[d - 1].start)

    for copy in qkv_copies:
        copy.wait()
    inc_s[...] = jnp.zeros_like(inc_s)
    for d in range(half - 1, 0, -1):

        @pl.when(place >= d)
        def _(d=d):
            end_copies[d - 1].wait_recv()
            through = ends_s[d - 1, tile[NS], :]
            for n in range(NS):
                inc_s[tile[n], :] = (
                    jnp.exp2(through * a_ref[tile[n], :]) * inc_s[tile[n], :]
                    + ends_s[d - 1, tile[n], :]
                )
            inc_s[tile[NS], :] = inc_s[tile[NS], :] + through

    first_copies = [
        pltpu.make_async_remote_copy(
            src_ref=all_s,
            dst_ref=first_s,
            send_sem=first_sem.at[1 + k],
            recv_sem=first_sem.at[0],
            device_id={"ctx": half + k},
            device_id_type=pl.DeviceIdType.MESH,
        )
        for k in range(group - half)
    ]

    @pl.when(slot == half - 1)
    def _():
        through = end_s[tile[NS], :]
        for n in range(NS):
            all_s[tile[n], :] = (
                jnp.exp2(through * a_ref[tile[n], :]) * inc_s[tile[n], :] + end_s[tile[n], :]
            )
        for copy in first_copies:
            copy.start()

    row = lax.broadcasted_iota(jnp.int32, (rows, rows), 0)
    col = lax.broadcasted_iota(jnp.int32, (rows, rows), 1)
    factor = HD**-0.5 * LOG2E
    outgoing = [
        pltpu.make_async_remote_copy(
            src_ref=o_s.at[i],
            dst_ref=back_s.at[slot],
            send_sem=out_sem.at[0, i],
            recv_sem=out_sem.at[1, slot],
            device_id={"ctx": i},
            device_id_type=pl.DeviceIdType.MESH,
        )
        for i in range(group)
    ]
    incoming = [
        pltpu.make_async_remote_copy(
            src_ref=o_s.at[i],
            dst_ref=back_s.at[i],
            send_sem=out_sem.at[0, i],
            recv_sem=out_sem.at[1, i],
            device_id={"ctx": i},
            device_id_type=pl.DeviceIdType.MESH,
        )
        for i in range(group)
    ]
    for i in range(group):
        q = got_s[i, 0]
        keys = got_s[: i + 1, 1].reshape((i + 1) * rows, HD)
        values = got_s[: i + 1, 2].reshape((i + 1) * rows, HD)
        s = lax.dot_general(
            q, keys, (((1,), (1,)), ((), ())), preferred_element_type=jnp.float32
        )
        last = jnp.where(col <= row, s[:, i * rows :], -jnp.inf)
        s = jnp.concatenate([s[:, : i * rows], last], axis=1) if i else last
        top = jnp.max(s, axis=1, keepdims=True)
        p = jnp.exp2((s - top) * factor)
        o = jnp.dot(p.astype(jnp.bfloat16), values, preferred_element_type=jnp.float32)
        o_s[i] = (o / jnp.sum(p, axis=1, keepdims=True)).astype(jnp.bfloat16)
        pl.when(slot != i)(outgoing[i].start)


    @pl.when(slot >= half)
    def _():
        first_copies[0].wait_recv()
        for n in range(NS):
            inc_s[tile[n], :] = (
                jnp.exp2(inc_s[tile[NS], :] * a_ref[tile[n], :]) * first_s[tile[n], :]
                + inc_s[tile[n], :]
            )

    def correct(block, carry):
        held = list(carry)
        for k in range(per):
            t = block * per + k
            at = pl.ds(pl.multiple_of(t * SUB, SUB), SUB)
            dt = d_s[at, :]
            sums = [y_s[at, :], None, None, None]
            for n in range(NS):
                held[n] = jnp.exp2(dt * a_ref[tile[n], :]) * held[n]
                term = held[n] * bc_s[NS + n, t]
                sums[n % 4] = term if sums[n % 4] is None else sums[n % 4] + term
            y_s[at, :] = (sums[0] + sums[1]) + (sums[2] + sums[3])
        return tuple(held)

    lax.fori_loop(0, rows // per, correct, tuple(inc_s[tile[n], :] for n in range(NS)))
    for c in range(SUB):
        cols = slice(c * LANES, (c + 1) * LANES)
        y = y_s[pl.ds(c, rows, stride=SUB), :] + skip_ref[:, cols] * x_ref[:, cols].astype(jnp.float32)
        g = gate_ref[:, cols].astype(jnp.float32)
        mix_ref[:, cols] = (y * (g / (1.0 + jnp.exp(-g)))).astype(mix_ref.dtype)

    att_ref[:, pl.ds(pl.multiple_of(slot * HD, HD), HD)] = o_s[slot]
    for i in range(group):

        @pl.when(slot != i)
        def _(i=i):
            outgoing[i].wait_send()
            incoming[i].wait_recv()
            att_ref[:, i * HD : (i + 1) * HD] = back_s[i]

    for d in range(1, half):
        pl.when(place + d < half)(end_copies[d - 1].wait_send)

    @pl.when(slot == half - 1)
    def _():
        for copy in first_copies:
            copy.wait_send()


def whole(query, key, value, xin, gate_z, delta, part, rate2, skip):
    rows, channels = xin.shape
    group, tp = lax.axis_size("ctx"), lax.axis_size("tp")
    f32, bf16 = jnp.float32, jnp.bfloat16
    tiles = pltpu.VMEM((rows * SUB, LANES), f32)
    ends = ((NS + 1) * SUB, LANES)
    return pl.pallas_call(
        functools.partial(whole_kernel, group, tp),
        out_shape=[jax.ShapeDtypeStruct((rows, channels), bf16)] * 2,
        in_specs=[VMEM] * 9,
        out_specs=[VMEM] * 2,
        scratch_shapes=[
            pltpu.VMEM((group - 1, 3, rows, HD), bf16),
            pltpu.VMEM((group, 3, rows, HD), bf16),
            pltpu.VMEM((tp - 1, 2 * NS, rows), f32),
            pltpu.VMEM((2 * NS, rows), f32),
            pltpu.SMEM((2 * NS, rows), f32),
            tiles,
            tiles,
            tiles,
            pltpu.VMEM(ends, f32),
            pltpu.VMEM((group // 2 - 1, *ends), f32),
            pltpu.VMEM(ends, f32),
            pltpu.VMEM((NS * SUB, LANES), f32),
            pltpu.VMEM((NS * SUB, LANES), f32),
            pltpu.VMEM((group, rows, HD), bf16),
            pltpu.VMEM((group, rows, HD), bf16),
            pltpu.SemaphoreType.DMA((2, tp - 1)),
            pltpu.SemaphoreType.DMA((2, group - 1)),
            pltpu.SemaphoreType.DMA((2, group // 2 - 1)),
            pltpu.SemaphoreType.DMA((1 + group // 2,)),
            pltpu.SemaphoreType.DMA((2, group)),
            pltpu.SemaphoreType.DMA,
        ],
        compiler_params=pltpu.CompilerParams(
            collective_id=0, has_side_effects=True, vmem_limit_bytes=40 * 1024 * 1024
        ),
    )(query, key, value, xin, gate_z, delta, part, rate2, skip)


def shards(query, key, value, xin, gate_z, w_bc, dt_low, dt_proj, dt_bias, a_rate, skip):
    rows, channels = xin.shape
    group = query.shape[1] // HD
    assert group * rows == WINDOW and lax.axis_size("ctx") % group == 0
    assert channels == SUB * LANES
    delta = jax.nn.softplus(
        jnp.dot(dt_low, dt_proj, preferred_element_type=jnp.float32) + dt_bias[None, :]
    )
    rate2 = (a_rate * -LOG2E).reshape(NS * SUB, LANES)
    if lax.axis_size("ctx") == group:
        part = lax.dot_general(
            w_bc, xin, (((0,), (1,)), ((), ())), preferred_element_type=jnp.float32
        )
        return tuple(whole(query, key, value, xin, gate_z, delta, part, rate2, skip[None, :]))
    packed = pack(query, key, value, group)
    partial_bc = jnp.dot(xin, w_bc, preferred_element_type=jnp.float32)
    tp = lax.axis_size("tp")
    others = [rotated(partial_bc, "tp", tp, d) for d in range(1, tp)]
    moved = [packed[0]] + [rotated(packed[d], "ctx", group, d) for d in range(1, group)]
    bc = sum(others, partial_bc)
    y, d, end = scan_block(delta, xin, rate2, bc)
    ends = earlier_ends(end, rate2)
    old = [shifted(block[1:], "ctx", group) for block in moved]
    outs = attention(moved, old, group)
    back = [outs[0]] + [rotated(outs[d], "ctx", group, d) for d in range(1, group)]
    mixed = finish(ends, y, d, rate2, bc, xin, gate_z, skip[None, :])
    return unpack(back, group), mixed


def solution(mesh):
    two = P("ctx", "tp")
    in_specs = (
        two,
        two,
        two,
        two,
        two,
        P("tp", None),
        P("ctx", None),
        P(None, "tp"),
        P("tp"),
        P(None, "tp"),
        P("tp"),
    )
    return jax.shard_map(
        shards, mesh=mesh, in_specs=in_specs, out_specs=(two, two), check_vma=False
    )
```

```python
import functools
import math

import jax
import jax.numpy as jnp
from jax import lax
from jax.experimental import pallas as pl
from jax.experimental.pallas import tpu as pltpu
from jax.sharding import PartitionSpec as P

HD = 128
WINDOW = 2048
NS = 16
LANES = 128
SUB = 8
LOG2E = math.log2(math.e)
RADIX = 8
VMEM = pl.BlockSpec(memory_space=pltpu.VMEM)
HBM = pl.BlockSpec(memory_space=pltpu.HBM)
SMEM = pl.BlockSpec(memory_space=pltpu.SMEM)
PARAMS = pltpu.CompilerParams(vmem_limit_bytes=40 * 1024 * 1024)


def shifted(block, axis, distance):
    peers = lax.axis_size(axis)
    return lax.ppermute(block, axis, [(i, i + distance) for i in range(peers - distance)])


def rotated(block, axis, group, distance):
    peers = lax.axis_size(axis)
    route = [(i, i // group * group + (i % group + distance) % group) for i in range(peers)]
    return lax.ppermute(block, axis, route)


def head_at(group, distance):
    slot = lax.rem(lax.axis_index("ctx"), group)
    return lax.rem(slot + distance + group, group)


def pack_kernel(group, q_ref, k_ref, v_ref, *outs):
    for d in range(group):
        col = pl.ds(pl.multiple_of(head_at(group, d) * HD, HD), HD)
        for part, ref in enumerate((q_ref, k_ref, v_ref)):
            outs[d][part] = ref[:, col]


def pack(query, key, value, group):
    rows = query.shape[0]
    return pl.pallas_call(
        functools.partial(pack_kernel, group),
        out_shape=[jax.ShapeDtypeStruct((3, rows, HD), query.dtype)] * group,
        in_specs=[VMEM] * 3,
        out_specs=[VMEM] * group,
        compiler_params=PARAMS,
        cost_estimate=pl.CostEstimate(flops=0, bytes_accessed=6 * query.size * 2, transcendentals=0),
    )(query, key, value)


def unpack_kernel(group, *refs):
    out = refs[group]
    for d in range(group):
        col = pl.ds(pl.multiple_of(head_at(group, -d) * HD, HD), HD)
        out[:, col] = refs[d][...]


def unpack(blocks, group):
    rows = blocks[0].shape[0]
    return pl.pallas_call(
        functools.partial(unpack_kernel, group),
        out_shape=jax.ShapeDtypeStruct((rows, group * HD), blocks[0].dtype),
        in_specs=[VMEM] * group,
        out_specs=VMEM,
        compiler_params=PARAMS,
        cost_estimate=pl.CostEstimate(flops=0, bytes_accessed=4 * rows * group * HD, transcendentals=0),
    )(*blocks)


def attention_kernel(group, rows, with_prev, *refs):
    sets = 2 if with_prev else 1
    outs = refs[sets * group : (sets + 1) * group]
    q_s, k_s, v_s, o_s = refs[(sets + 1) * group :]
    base = group * rows if with_prev else 0
    for d in range(group):
        at = head_at(group, -d) * rows
        src = refs[d]
        q_s[pl.ds(pl.multiple_of(at, rows), rows), :] = src[0]
        k_s[pl.ds(pl.multiple_of(base + at, rows), rows), :] = src[1]
        v_s[pl.ds(pl.multiple_of(base + at, rows), rows), :] = src[2]
        if with_prev:
            old = refs[group + d]
            k_s[pl.ds(pl.multiple_of(at, rows), rows), :] = old[0]
            v_s[pl.ds(pl.multiple_of(at, rows), rows), :] = old[1]
    row = lax.broadcasted_iota(jnp.int32, (rows, rows), 0)
    col = lax.broadcasted_iota(jnp.int32, (rows, rows), 1)
    factor = HD**-0.5 * LOG2E
    for i in range(group):
        lo = i * rows if with_prev else 0
        hi = base + (i + 1) * rows
        q = q_s[i * rows : (i + 1) * rows, :]
        s = lax.dot_general(
            q, k_s[lo:hi, :], (((1,), (1,)), ((), ())), preferred_element_type=jnp.float32
        )
        last = jnp.where(col <= row, s[:, hi - lo - rows :], -jnp.inf)
        parts = [s[:, : hi - lo - rows], last] if hi - lo > rows else [last]
        if with_prev:
            held = lax.axis_index("ctx") >= group
            middle = s[:, rows : hi - lo - rows]
            first = jnp.where((col > row) & held, s[:, :rows], -jnp.inf)
            number = lax.broadcasted_iota(jnp.int32, middle.shape, 1) + (lo + rows)
            middle = jnp.where((number >= base) | held, middle, -jnp.inf)
            parts = [first, middle, last]
        s = jnp.concatenate(parts, axis=1) if len(parts) > 1 else parts[0]
        top = jnp.max(s, axis=1, keepdims=True)
        p = jnp.exp2((s - top) * factor)
        total = jnp.sum(p, axis=1, keepdims=True)
        o = jnp.dot(p.astype(jnp.bfloat16), v_s[lo:hi, :], preferred_element_type=jnp.float32)
        o_s[i * rows : (i + 1) * rows, :] = (o / total).astype(jnp.bfloat16)
    for d in range(group):
        at = head_at(group, d) * rows
        outs[d][...] = o_s[pl.ds(pl.multiple_of(at, rows), rows), :]


def attention(blocks, old, group):
    rows = blocks[0].shape[1]
    with_prev = old is not None
    length = group * rows
    keys = length * (2 if with_prev else 1)
    operands = list(blocks) + (list(old) if with_prev else [])
    bf16 = jnp.bfloat16
    return pl.pallas_call(
        functools.partial(attention_kernel, group, rows, with_prev),
        out_shape=[jax.ShapeDtypeStruct((rows, HD), bf16)] * group,
        in_specs=[VMEM] * len(operands),
        out_specs=[VMEM] * group,
        scratch_shapes=[
            pltpu.VMEM((length, HD), bf16),
            pltpu.VMEM((keys, HD), bf16),
            pltpu.VMEM((keys, HD), bf16),
            pltpu.VMEM((length, HD), bf16),
        ],
        compiler_params=PARAMS,
        cost_estimate=pl.CostEstimate(
            flops=2 * length * keys * HD,
            bytes_accessed=8 * length * HD,
            transcendentals=length * keys // 2,
        ),
    )(*operands)


def scan_kernel(delta_ref, x_ref, a_ref, bc_ref, y_ref, d_ref, end_ref, u_s):
    rows = delta_ref.shape[0]
    for c in range(SUB):
        cols = slice(c * LANES, (c + 1) * LANES)
        dt = delta_ref[:, cols]
        d_ref[pl.ds(c, rows, stride=SUB), :] = dt
        u_s[pl.ds(c, rows, stride=SUB), :] = dt * x_ref[:, cols].astype(jnp.float32)

    per = 4

    def step(block, carry):
        states, through = list(carry[:NS]), carry[NS]
        for k in range(per):
            t = block * per + k
            at = pl.ds(pl.multiple_of(t * SUB, SUB), SUB)
            dt, u = d_ref[at, :], u_s[at, :]
            through = through + dt
            sums = [None] * 4
            for n in range(NS):
                e = jnp.exp2(dt * a_ref[n * SUB : (n + 1) * SUB, :])
                states[n] = e * states[n] + u * bc_ref[t, n]
                term = states[n] * bc_ref[t, NS + n]
                sums[n % 4] = term if n < 4 else sums[n % 4] + term
            y_ref[at, :] = (sums[0] + sums[1]) + (sums[2] + sums[3])
        return (*states, through)

    zero = jnp.zeros((SUB, LANES), jnp.float32)
    ends = lax.fori_loop(0, rows // per, step, (zero,) * (NS + 1))
    for n in range(NS + 1):
        end_ref[n * SUB : (n + 1) * SUB, :] = ends[n]


def scan_block(delta, x, rate2, bc):
    rows, channels = delta.shape
    f32 = jnp.float32
    tiles = jax.ShapeDtypeStruct((rows * SUB, LANES), f32)
    return pl.pallas_call(
        scan_kernel,
        out_shape=[tiles, tiles, jax.ShapeDtypeStruct(((NS + 1) * SUB, LANES), f32)],
        in_specs=[VMEM, VMEM, VMEM, SMEM],
        out_specs=[VMEM] * 3,
        scratch_shapes=[pltpu.VMEM((rows * SUB, LANES), f32)],
        compiler_params=PARAMS,
        cost_estimate=pl.CostEstimate(
            flops=200 * rows * channels * NS,
            bytes_accessed=14 * rows * channels,
            transcendentals=rows * channels * NS,
        ),
    )(delta, x, rate2, bc)


def finish_kernel(count, *refs):
    ends = refs[:count]
    y_ref, d_ref, a_ref, bc_ref, x_ref, gate_ref, skip_ref, out_ref, y_s = refs[count:]
    rows = x_ref.shape[0]
    tile = [slice(n * SUB, (n + 1) * SUB) for n in range(NS + 1)]
    states = [jnp.zeros((SUB, LANES), jnp.float32)] * NS
    for end in ends:
        through = end[tile[NS], :]
        states = [
            jnp.exp2(through * a_ref[tile[n], :]) * states[n] + end[tile[n], :] for n in range(NS)
        ]
    per = 4

    def step(block, carry):
        held = list(carry)
        for k in range(per):
            t = block * per + k
            at = pl.ds(pl.multiple_of(t * SUB, SUB), SUB)
            dt = d_ref[at, :]
            sums = [y_ref[at, :], None, None, None]
            for n in range(NS):
                held[n] = jnp.exp2(dt * a_ref[tile[n], :]) * held[n]
                term = held[n] * bc_ref[t, NS + n]
                sums[n % 4] = term if sums[n % 4] is None else sums[n % 4] + term
            y_s[at, :] = (sums[0] + sums[1]) + (sums[2] + sums[3])
        return tuple(held)

    lax.fori_loop(0, rows // per, step, tuple(states))
    for c in range(SUB):
        cols = slice(c * LANES, (c + 1) * LANES)
        y = y_s[pl.ds(c, rows, stride=SUB), :] + skip_ref[:, cols] * x_ref[:, cols].astype(jnp.float32)
        g = gate_ref[:, cols].astype(jnp.float32)
        out_ref[:, cols] = (y * (g / (1.0 + jnp.exp(-g)))).astype(out_ref.dtype)


def finish(ends, y, d, rate2, bc, x, gate, skip):
    rows, channels = x.shape
    return pl.pallas_call(
        functools.partial(finish_kernel, len(ends)),
        out_shape=jax.ShapeDtypeStruct((rows, channels), jnp.bfloat16),
        in_specs=[VMEM] * len(ends) + [VMEM, VMEM, VMEM, SMEM, VMEM, VMEM, VMEM],
        out_specs=VMEM,
        scratch_shapes=[pltpu.VMEM((rows * SUB, LANES), jnp.float32)],
        compiler_params=PARAMS,
        cost_estimate=pl.CostEstimate(
            flops=150 * rows * channels * NS,
            bytes_accessed=14 * rows * channels,
            transcendentals=rows * channels * NS,
        ),
    )(*ends, y, d, rate2, bc, x, gate, skip)


def joined(later, earlier, rate2):
    cut = NS * SUB
    through = jnp.tile(later[cut:], (NS, 1))
    state = jnp.exp2(through * rate2) * earlier[:cut] + later[:cut]
    return jnp.concatenate([state, later[cut:] + earlier[cut:]], axis=0)


def earlier_ends(end, rate2):
    peers = lax.axis_size("ctx")
    whole, span = end, 1
    while span < peers:
        away = [d * span for d in range(1, RADIX) if d * span < peers]
        parts = [shifted(whole, "ctx", d) for d in away]
        for part in parts:
            whole = joined(whole, part, rate2)
        span *= RADIX
    return [shifted(whole, "ctx", 1)]


def send(src, dst, sems, at, axis, peer):
    return pltpu.make_async_remote_copy(
        src_ref=src,
        dst_ref=dst,
        send_sem=sems.at[0, at],
        recv_sem=sems.at[1, at],
        device_id={axis: peer},
        device_id_type=pl.DeviceIdType.MESH,
    )


def whole_kernel(group, tp, *refs):
    q_ref, k_ref, v_ref, x_hbm, gate_hbm, proj_hbm, low_ref, w_ref, bias_ref, a_ref, skip_ref = refs[:11]
    att_ref, mix_ref = refs[11:13]
    x_ref, gate_ref, proj_ref, part_ref = refs[13:17]
    (pack_s, got_s, bcs_s, bc_v, bc_s, y_s, d_s, u_s, end_s, ends_s) = refs[17:27]
    inc_s, all_s, first_s, o_s, back_s = refs[27:32]
    bc_sem, qkv_sem, end_sem, first_sem, out_sem, copy_sem, load_sem, side_sem = refs[32:]
    rows = x_ref.shape[0]
    slot = lax.axis_index("ctx")
    line = lax.axis_index("tp")
    peer = [lax.rem(slot + d, group) for d in range(group)]

    barrier = pltpu.get_barrier_semaphore()
    for d in range(1, group):
        pl.semaphore_signal(
            barrier, inc=1, device_id={"ctx": peer[d]}, device_id_type=pl.DeviceIdType.MESH
        )
    for d in range(1, tp):
        pl.semaphore_signal(
            barrier,
            inc=1,
            device_id={"tp": lax.rem(line + d, tp)},
            device_id_type=pl.DeviceIdType.MESH,
        )
    loads = []
    for d in (*range(1, group), 0):
        col = pl.ds(pl.multiple_of(peer[d] * HD, HD), HD)
        room = pack_s.at[d - 1] if d else got_s.at[slot]
        for part, ref in enumerate((q_ref, k_ref, v_ref)):
            loads.append(
                pltpu.make_async_copy(ref.at[:, col], room.at[part], load_sem.at[d, part])
            )
    sides = [
        pltpu.make_async_copy(src, dst, side_sem.at[k])
        for k, (src, dst) in enumerate(
            ((x_hbm, x_ref), (proj_hbm, proj_ref), (gate_hbm, gate_ref))
        )
    ]
    for copy in loads[:3] + sides[:1] + loads[3:] + sides[1:]:
        copy.start()
    pl.semaphore_wait(barrier, group + tp - 2)

    qkv_out = [
        pltpu.make_async_remote_copy(
            src_ref=pack_s.at[d - 1],
            dst_ref=got_s.at[slot],
            send_sem=qkv_sem.at[0, d],
            recv_sem=qkv_sem.at[1, slot],
            device_id={"ctx": peer[d]},
            device_id_type=pl.DeviceIdType.MESH,
        )
        for d in range(1, group)
    ]
    qkv_in = [
        pltpu.make_async_remote_copy(
            src_ref=pack_s.at[0],
            dst_ref=got_s.at[i],
            send_sem=qkv_sem.at[0, 1],
            recv_sem=qkv_sem.at[1, i],
            device_id={"ctx": peer[1]},
            device_id_type=pl.DeviceIdType.MESH,
        )
        for i in range(group)
    ]
    for d in range(1, group):
        for copy in loads[3 * d - 3 : 3 * d]:
            copy.wait()
        qkv_out[d - 1].start()
    sides[0].wait()
    part_ref[...] = lax.dot_general(
        w_ref[...], x_ref[...], (((1,), (1,)), ((), ())), preferred_element_type=jnp.float32
    )
    bc_copies = [
        send(part_ref, bcs_s.at[d - 1], bc_sem, d - 1, "tp", lax.rem(line + d, tp))
        for d in range(1, tp)
    ]
    for copy in bc_copies:
        copy.start()
    for copy in loads[3 * group - 3 :]:
        copy.wait()
    sides[1].wait()

    for c in range(SUB):
        cols = slice(c * LANES, (c + 1) * LANES)
        raw = bias_ref[:, cols] + jnp.dot(
            low_ref[...], proj_ref[:, cols], preferred_element_type=jnp.float32
        )
        z = jnp.exp(-jnp.abs(raw))
        w = 1.0 + z
        tiny = w == 1.0
        dt = jnp.maximum(raw, 0.0) + jnp.where(
            tiny, z, jnp.log(w) * (z / jnp.where(tiny, 1.0, w - 1.0))
        )
        d_s[pl.ds(c, rows, stride=SUB), :] = dt
        u_s[pl.ds(c, rows, stride=SUB), :] = dt * x_ref[:, cols].astype(jnp.float32)
    total = part_ref[...]
    for d in range(1, tp):
        bc_copies[d - 1].wait()
        total = total + bcs_s[d - 1]
    bc_v[...] = total
    to_scalars = pltpu.make_async_copy(bc_v, bc_s, copy_sem)
    to_scalars.start()
    to_scalars.wait()

    tile = [slice(n * SUB, (n + 1) * SUB) for n in range(NS + 1)]
    per = 4

    def step(block, carry):
        states, through = list(carry[:NS]), carry[NS]
        for k in range(per):
            t = block * per + k
            at = pl.ds(pl.multiple_of(t * SUB, SUB), SUB)
            dt, u = d_s[at, :], u_s[at, :]
            through = through + dt
            sums = [None] * 4
            for n in range(NS):
                e = jnp.exp2(dt * a_ref[tile[n], :])
                states[n] = e * states[n] + u * bc_s[n, t]
                term = states[n] * bc_s[NS + n, t]
                sums[n % 4] = term if n < 4 else sums[n % 4] + term
            y_s[at, :] = (sums[0] + sums[1]) + (sums[2] + sums[3])
        return (*states, through)

    zero = jnp.zeros((SUB, LANES), jnp.float32)
    ends = lax.fori_loop(0, rows // per, step, (zero,) * (NS + 1))
    for n in range(NS + 1):
        end_s[tile[n], :] = ends[n]

    half = group // 2
    place = lax.rem(slot, half)
    end_copies = [
        send(end_s, ends_s.at[d - 1], end_sem, d - 1, "ctx", peer[d]) for d in range(1, half)
    ]
    for d in range(1, half):
        pl.when(place + d < half)(end_copies[d - 1].start)

    row = lax.broadcasted_iota(jnp.int32, (rows, rows), 0)
    col = lax.broadcasted_iota(jnp.int32, (rows, rows), 1)
    factor = HD**-0.5 * LOG2E
    outgoing = [
        pltpu.make_async_remote_copy(
            src_ref=o_s.at[i],
            dst_ref=back_s.at[slot],
            send_sem=out_sem.at[0, i],
            recv_sem=out_sem.at[1, slot],
            device_id={"ctx": i},
            device_id_type=pl.DeviceIdType.MESH,
        )
        for i in range(group)
    ]
    incoming = [
        pltpu.make_async_remote_copy(
            src_ref=o_s.at[i],
            dst_ref=back_s.at[i],
            send_sem=out_sem.at[0, i],
            recv_sem=out_sem.at[1, i],
            device_id={"ctx": i},
            device_id_type=pl.DeviceIdType.MESH,
        )
        for i in range(group)
    ]
    for i in range(group):
        pl.when(slot != i)(qkv_in[i].wait_recv)
        q = got_s[i, 0]
        keys = got_s[: i + 1, 1].reshape((i + 1) * rows, HD)
        values = got_s[: i + 1, 2].reshape((i + 1) * rows, HD)
        s = lax.dot_general(
            q, keys, (((1,), (1,)), ((), ())), preferred_element_type=jnp.float32
        )
        last = jnp.where(col <= row, s[:, i * rows :], -jnp.inf)
        s = jnp.concatenate([s[:, : i * rows], last], axis=1) if i else last
        top = jnp.max(s, axis=1, keepdims=True)
        p = jnp.exp2((s - top) * factor)
        o = jnp.dot(p.astype(jnp.bfloat16), values, preferred_element_type=jnp.float32)
        o_s[i] = (o / jnp.sum(p, axis=1, keepdims=True)).astype(jnp.bfloat16)
        pl.when(slot != i)(outgoing[i].start)
        if i == half - 1:
            inc_s[...] = jnp.zeros_like(inc_s)
            for d in range(half - 1, 0, -1):

                @pl.when(place >= d)
                def _(d=d):
                    end_copies[d - 1].wait_recv()
                    through = ends_s[d - 1, tile[NS], :]
                    for n in range(NS):
                        inc_s[tile[n], :] = (
                            jnp.exp2(through * a_ref[tile[n], :]) * inc_s[tile[n], :]
                            + ends_s[d - 1, tile[n], :]
                        )
                    inc_s[tile[NS], :] = inc_s[tile[NS], :] + through

            first_copies = [
                pltpu.make_async_remote_copy(
                    src_ref=all_s,
                    dst_ref=first_s,
                    send_sem=first_sem.at[1 + k],
                    recv_sem=first_sem.at[0],
                    device_id={"ctx": half + k},
                    device_id_type=pl.DeviceIdType.MESH,
                )
                for k in range(group - half)
            ]

            @pl.when(slot == half - 1)
            def _():
                through = end_s[tile[NS], :]
                for n in range(NS):
                    all_s[tile[n], :] = (
                        jnp.exp2(through * a_ref[tile[n], :]) * inc_s[tile[n], :] + end_s[tile[n], :]
                    )
                for copy in first_copies:
                    copy.start()

    @pl.when(slot >= half)
    def _():
        first_copies[0].wait_recv()
        for n in range(NS):
            inc_s[tile[n], :] = (
                jnp.exp2(inc_s[tile[NS], :] * a_ref[tile[n], :]) * first_s[tile[n], :]
                + inc_s[tile[n], :]
            )

    def correct(block, carry):
        held = list(carry)
        for k in range(per):
            t = block * per + k
            at = pl.ds(pl.multiple_of(t * SUB, SUB), SUB)
            dt = d_s[at, :]
            sums = [y_s[at, :], None, None, None]
            for n in range(NS):
                held[n] = jnp.exp2(dt * a_ref[tile[n], :]) * held[n]
                term = held[n] * bc_s[NS + n, t]
                sums[n % 4] = term if sums[n % 4] is None else sums[n % 4] + term
            y_s[at, :] = (sums[0] + sums[1]) + (sums[2] + sums[3])
        return tuple(held)

    lax.fori_loop(0, rows // per, correct, tuple(inc_s[tile[n], :] for n in range(NS)))
    sides[2].wait()
    for c in range(SUB):
        cols = slice(c * LANES, (c + 1) * LANES)
        y = y_s[pl.ds(c, rows, stride=SUB), :] + skip_ref[:, cols] * x_ref[:, cols].astype(jnp.float32)
        g = gate_ref[:, cols].astype(jnp.float32)
        mix_ref[:, cols] = (y * (g / (1.0 + jnp.exp(-g)))).astype(mix_ref.dtype)

    att_ref[:, pl.ds(pl.multiple_of(slot * HD, HD), HD)] = o_s[slot]
    for i in range(group):

        @pl.when(slot != i)
        def _(i=i):
            outgoing[i].wait_send()
            incoming[i].wait_recv()
            att_ref[:, i * HD : (i + 1) * HD] = back_s[i]

    for copy in qkv_out:
        copy.wait_send()
    for d in range(1, half):
        pl.when(place + d < half)(end_copies[d - 1].wait_send)

    @pl.when(slot == half - 1)
    def _():
        for copy in first_copies:
            copy.wait_send()


def whole(query, key, value, xin, gate_z, dt_proj, dt_low, w_rows, dt_bias, rate2, skip):
    rows, channels = xin.shape
    group, tp = lax.axis_size("ctx"), lax.axis_size("tp")
    f32, bf16 = jnp.float32, jnp.bfloat16
    tiles = pltpu.VMEM((rows * SUB, LANES), f32)
    ends = ((NS + 1) * SUB, LANES)
    return pl.pallas_call(
        functools.partial(whole_kernel, group, tp),
        out_shape=[jax.ShapeDtypeStruct((rows, channels), bf16)] * 2,
        in_specs=[HBM] * 6 + [VMEM] * 5,
        out_specs=[VMEM] * 2,
        scratch_shapes=[
            pltpu.VMEM((rows, channels), bf16),
            pltpu.VMEM((rows, channels), bf16),
            pltpu.VMEM(dt_proj.shape, bf16),
            pltpu.VMEM((2 * NS, rows), f32),
            pltpu.VMEM((group - 1, 3, rows, HD), bf16),
            pltpu.VMEM((group, 3, rows, HD), bf16),
            pltpu.VMEM((tp - 1, 2 * NS, rows), f32),
            pltpu.VMEM((2 * NS, rows), f32),
            pltpu.SMEM((2 * NS, rows), f32),
            tiles,
            tiles,
            tiles,
            pltpu.VMEM(ends, f32),
            pltpu.VMEM((group // 2 - 1, *ends), f32),
            pltpu.VMEM(ends, f32),
            pltpu.VMEM((NS * SUB, LANES), f32),
            pltpu.VMEM((NS * SUB, LANES), f32),
            pltpu.VMEM((group, rows, HD), bf16),
            pltpu.VMEM((group, rows, HD), bf16),
            pltpu.SemaphoreType.DMA((2, tp - 1)),
            pltpu.SemaphoreType.DMA((2, group)),
            pltpu.SemaphoreType.DMA((2, group // 2 - 1)),
            pltpu.SemaphoreType.DMA((1 + group // 2,)),
            pltpu.SemaphoreType.DMA((2, group)),
            pltpu.SemaphoreType.DMA,
            pltpu.SemaphoreType.DMA((group, 3)),
            pltpu.SemaphoreType.DMA((3,)),
        ],
        compiler_params=pltpu.CompilerParams(
            collective_id=0, has_side_effects=True, vmem_limit_bytes=60 * 1024 * 1024
        ),
    )(query, key, value, xin, gate_z, dt_proj, dt_low, w_rows, dt_bias, rate2, skip)


def shards(query, key, value, xin, gate_z, w_bc, dt_low, dt_proj, dt_bias, a_rate, skip):
    rows, channels = xin.shape
    group = query.shape[1] // HD
    assert group * rows == WINDOW and lax.axis_size("ctx") % group == 0
    assert channels == SUB * LANES
    rate2 = (a_rate * -LOG2E).reshape(NS * SUB, LANES)
    if lax.axis_size("ctx") == group:
        return tuple(
            whole(
                query, key, value, xin, gate_z, dt_proj, dt_low, w_bc.T, dt_bias[None, :], rate2,
                skip[None, :],
            )
        )
    delta = jax.nn.softplus(
        jnp.dot(dt_low, dt_proj, preferred_element_type=jnp.float32) + dt_bias[None, :]
    )
    packed = pack(query, key, value, group)
    partial_bc = jnp.dot(xin, w_bc, preferred_element_type=jnp.float32)
    tp = lax.axis_size("tp")
    others = [rotated(partial_bc, "tp", tp, d) for d in range(1, tp)]
    moved = [packed[0]] + [rotated(packed[d], "ctx", group, d) for d in range(1, group)]
    bc = sum(others, partial_bc)
    y, d, end = scan_block(delta, xin, rate2, bc)
    ends = earlier_ends(end, rate2)
    old = [shifted(block[1:], "ctx", group) for block in moved]
    outs = attention(moved, old, group)
    back = [outs[0]] + [rotated(outs[d], "ctx", group, d) for d in range(1, group)]
    mixed = finish(ends, y, d, rate2, bc, xin, gate_z, skip[None, :])
    return unpack(back, group), mixed


def solution(mesh):
    two = P("ctx", "tp")
    in_specs = (
        two,
        two,
        two,
        two,
        two,
        P("tp", None),
        P("ctx", None),
        P(None, "tp"),
        P("tp"),
        P(None, "tp"),
        P("tp"),
    )
    return jax.shard_map(
        shards, mesh=mesh, in_specs=in_specs, out_specs=(two, two), check_vma=False
    )
```
